32 devices in a mesh: groups: 2 (over x), rows: 8 (over z, y), cols: 2 (over core).
Axes of the slice: x: 2, y: 2, z: 4, core: 2. Of those that a mesh axis runs over, the one named last changes fastest.
Arguments:
- embeddings: float32 [8192, 768], P(('groups', 'rows', 'cols')), parts along dimension 0
- cluster_size: int32 [8], P('groups'), parts along dimension 0, may hold values from 192 to 3072, as said below
- cluster_start: int32 [8], P('groups'), parts along dimension 0, may hold values from 0 to 3904, as said below
- live: int32 [8192], P(('groups', 'rows', 'cols')), parts along dimension 0, may hold values 0 or 1
Outputs:
- best: float32 [8192], P(('groups', 'rows', 'cols')), parts along dimension 0
The draws below stay inside these ranges and needn't reach their ends.
There are 2 independent parts, one for each index of `groups`. The reference program is written for one: setup_inputs(seed, part) draws one part's arguments, and reference() takes and returns one part's arrays. A program takes and returns all parts, laid end to end along the dimension named above; each array names one. Nothing has to cross between parts.
Inputs may be any that keep to these rules, and one draw needn't show every extreme that they name: `cluster_size`: clusters are disjoint ranges of rows within the 4096 rows, each of 192 members or more; one of them has exactly 3072 members. Each cluster_start[k] + cluster_size[k] is at most 4096.
All inputs are finite; a program needn't handle non-finite values. No bound on the sum of `live` on one device may be relied on, other than what follows from the above.
Results may differ from the reference program's by a relative error of at most 0.00062.
Values may be sent and summed in bfloat16 or wider, within the bound.
No kernel may reach another device: no remote copies, remote signals or barrier semaphores. Data moves between devices by JAX's collectives and lax.ppermute only.
A program may use at most 64 MiB of HBM per device.

```python
import jax
import jax.numpy as jnp
from jax import lax

E = 768
CLUSTERS = 4
MEMBER_ROWS = 4096
MOST = 3072


def layout(key):
    key = jax.random.fold_in(key, 11)
    first, second, third = jax.random.split(key, 3)
    others = jax.random.randint(first, (CLUSTERS - 1,), MOST // 16, (MEMBER_ROWS - MOST) // 3 + 1)
    sizes = jnp.concatenate([jnp.array([MOST], jnp.int32), others.astype(jnp.int32)])
    sizes = jax.random.permutation(second, sizes)
    spare = MEMBER_ROWS - jnp.sum(sizes)
    gaps = jax.random.randint(third, (CLUSTERS,), 0, spare // CLUSTERS + 1).astype(jnp.int32)
    starts = jnp.cumsum(gaps + sizes) - sizes
    return (sizes.astype(jnp.int32), starts.astype(jnp.int32))


def draw_cluster_size(key, part):
    sizes, starts = layout(key)
    return sizes


def draw_cluster_start(key, part):
    sizes, starts = layout(key)
    return starts


def draw_embeddings(key, part):
    sizes, starts = layout(key)
    key = jax.random.fold_in(key, 5)
    noise_random_key, common_random_key, weight_random_key, scale_random_key = jax.random.split(key, 4)
    rowid = jnp.arange(MEMBER_ROWS, dtype=jnp.int32)
    inside = (rowid[:, None] >= starts[None, :]) & (rowid[:, None] < starts[None, :] + sizes[None, :])
    start_of = jnp.sum(jnp.where(inside, starts[None, :], 0), axis=1)
    member = jnp.any(inside, axis=1)
    offset = rowid - start_of
    share = jnp.where(member, start_of + offset % (MEMBER_ROWS // 2), rowid)
    weight = jax.random.uniform(weight_random_key, (MEMBER_ROWS, 1), jnp.float32, 0.25, 0.85)
    common = jax.random.normal(common_random_key, (MEMBER_ROWS, E), jnp.float32)[share]
    noise = jax.random.normal(noise_random_key, (MEMBER_ROWS, E), jnp.float32)
    scale_factor = jnp.exp(jax.random.uniform(scale_random_key, (MEMBER_ROWS, 1), jnp.float32, 0.0, 2.3))
    rows_out = weight * common + jnp.sqrt(1.0 - weight * weight) * noise
    return (scale_factor * rows_out).astype(jnp.float32)


def set_ends(values, rng, low, top_value):
    place = [jax.random.randint(jax.random.fold_in(rng, axis), (), 0, length) for axis, length in enumerate(values.shape)]
    longest = values.shape.index(max(values.shape))
    beside = place[:longest] + [(place[longest] + 1) % values.shape[longest]] + place[longest + 1:]
    return values.at[tuple(place)].set(low).at[tuple(beside)].set(top_value)


def setup_inputs(seed: int = 0, part: int = 0) -> dict:
    splits = jax.random.split(jax.random.key(seed), 5)
    part_keys = jax.random.split(jax.random.fold_in(splits[4], part), 5)
    embeddings = draw_embeddings(jax.random.fold_in(jax.random.fold_in(splits[4], part), 71), part)
    cluster_size = draw_cluster_size(jax.random.fold_in(jax.random.fold_in(splits[4], part), 71), part)
    cluster_start = draw_cluster_start(jax.random.fold_in(jax.random.fold_in(splits[4], part), 71), part)
    live = set_ends((jax.random.randint(part_keys[3], (MEMBER_ROWS,), 0, 8) < 7).astype(jnp.int32), jax.random.fold_in(part_keys[3], 1), 0, 1)
    return dict(embeddings=embeddings, cluster_size=cluster_size, cluster_start=cluster_start, live=live)


def labels_of(gid, cluster_size, cluster_start):
    inside = (gid[:, None] >= cluster_start[None, :]) & (gid[:, None] < cluster_start[None, :] + cluster_size[None, :])
    ids = jnp.arange(cluster_size.shape[0], dtype=jnp.int32)
    return lax.optimization_barrier(jnp.max(jnp.where(inside, ids[None, :], -1), axis=1)).astype(jnp.int32)

def reference(embeddings, cluster_size, cluster_start, live):
    squares = lax.optimization_barrier(jnp.sum(embeddings * embeddings, axis=1, keepdims=True))
    normed = (embeddings * lax.rsqrt(squares + 1e-06)).astype(jnp.bfloat16)
    gid = jnp.arange(MEMBER_ROWS, dtype=jnp.int32)
    label = labels_of(gid, cluster_size, cluster_start)
    key_label = jnp.where((live == 1) & (label >= 0), label, -2).astype(jnp.int32)
    block = MEMBER_ROWS // 16

    def one_block(index):
        first = (index * block).astype(jnp.int32)
        queries = lax.dynamic_slice_in_dim(normed, first, block, 0)
        qlab = lax.dynamic_slice_in_dim(label, first, block, 0)
        qgid = first + jnp.arange(block, dtype=jnp.int32)
        sim = jnp.dot(queries, normed.T, preferred_element_type=jnp.float32)
        valid = (qlab[:, None] == key_label[None, :]) & (qgid[:, None] != gid[None, :])
        return lax.optimization_barrier(jnp.max(jnp.where(valid, sim, jnp.float32(-2.0)), axis=1))
    peak = lax.map(one_block, jnp.arange(16, dtype=jnp.int32)).reshape(MEMBER_ROWS)
    return jnp.where((live == 1) & (peak > -1.5), peak, jnp.float32(0.0))
```

```python
import functools

import jax
import jax.numpy as jnp
import numpy as np
from jax import lax
from jax.experimental import pallas as pl
from jax.experimental.pallas import tpu as pltpu
from jax.sharding import PartitionSpec as P

AXES = ("rows", "cols")
EMPTY = -2.0

GRID8 = ((2,), (0, 3), (1, 4, 6), (2, 5), (0, 5, 6), (1, 2, 7), (), (3, 4, 6))


def held_sets(chips):
    if chips == 8:
        return GRID8
    cover, seen = [0], {0}
    while len(seen) < chips:
        gain, step = max(
            (len({(s - c) % chips for c in cover} | {(c - s) % chips for c in cover} | seen), -s)
            for s in range(1, chips)
            if s not in cover
        )
        cover.append(-step)
        seen = {(a - b) % chips for a in cover for b in cover}
    return tuple(tuple((c + d) % chips for d in cover[1:]) for c in range(chips))


def steps_of(sets):
    edges = [(s, t) for t, held in enumerate(sets) for s in held]
    n = len(sets)
    degree = max(
        [sum(e[0] == c for e in edges) for c in range(n)] + [sum(e[1] == c for e in edges) for c in range(n)]
    )
    out = [[None] * degree for _ in range(n)]
    inn = [[None] * degree for _ in range(n)]
    color = {}
    for s, t in edges:
        a = out[s].index(None)
        b = inn[t].index(None)
        if a != b:
            path, node, side, want = [], t, 1, a
            while True:
                e = (inn if side else out)[node][want]
                if e is None:
                    break
                path.append(e)
                node = e[0] if side else e[1]
                side, want = 1 - side, a + b - want
            for e in path:
                out[e[0]][color[e]] = inn[e[1]][color[e]] = None
            for e in path:
                color[e] = a + b - color[e]
                out[e[0]][color[e]] = inn[e[1]][color[e]] = e
        color[(s, t)] = a
        out[s][a] = inn[t][a] = (s, t)
    return [[e for e in edges if color[e] == k] for k in range(degree)]


@functools.lru_cache(None)
def plan(chips, rows_dev):
    sets = held_sets(chips)
    steps = steps_of(sets)
    slots = 2 + 2 * len(steps)
    blocks = np.full((2 * chips, slots), -1, np.int32)
    for c in range(chips):
        for core in range(2):
            blocks[2 * c + core, 0] = 2 * c + core
            blocks[2 * c + core, 1] = 2 * c + 1 - core
            for k, step in enumerate(steps):
                for s, t in step:
                    if t == c:
                        blocks[2 * c + core, 2 + 2 * k] = 2 * s + core
                        blocks[2 * c + core, 3 + 2 * k] = 2 * s + 1 - core
    total = 2 * chips
    largest = total * rows_dev * 3 // 4
    work = [[] for _ in range(total)]
    wanted = []
    for a in range(total):
        for b in range(a + 1, total):
            if (b - a - 1) * rows_dev + 1 >= largest:
                continue
            able = [d for d in range(total) if a in blocks[d] and b in blocks[d]]
            assert able, (a, b)
            wanted.append((len(able), a, b, able))
    for _, a, b, able in sorted(wanted):
        d = min(able, key=lambda d: (len(work[d]), d))
        work[d].append((a, b))
    most = max(len(w) for w in work)
    table = np.zeros((total, slots + 1 + 2 * most), np.int32)
    for d in range(total):
        row = list(blocks[d])
        table[d, :slots] = blocks[d]
        table[d, slots] = len(work[d])
        for i, (a, b) in enumerate(work[d]):
            table[d, slots + 1 + 2 * i] = row.index(a)
            table[d, slots + 2 + 2 * i] = row.index(b)
    return steps, table


def labels(gid, size_ref, start_ref):
    label = jnp.full(gid.shape, -1, jnp.int32)
    for k in range(size_ref.shape[0]):
        first = start_ref[k]
        label = jnp.where((gid >= first) & (gid < first + size_ref[k]), k, label)
    return label


def my_block():
    return lax.axis_index("rows") * lax.axis_size("cols") + lax.axis_index("cols")


def norm_kernel(size_ref, start_ref, live_ref, emb_ref, out_ref):
    rows, width = emb_ref.shape
    emb = emb_ref[...]
    squares = jnp.sum(emb * emb, axis=1, keepdims=True)
    normed = emb * lax.rsqrt(squares + 1e-06)
    gid = my_block() * rows + lax.broadcasted_iota(jnp.int32, (1, rows), 1)
    member = labels(gid, size_ref, start_ref) >= 0
    counts = jnp.where(member & (live_ref[...] == 1), jnp.float32(1), jnp.float32(0))
    counts = jnp.broadcast_to(counts, (128, rows)).T[:, :1]
    out_ref[...] = jnp.where(counts > 0, normed, jnp.float32(jnp.nan)).astype(out_ref.dtype)


def pair_kernel(slots, table_ref, size_ref, start_ref, *refs):
    ins, outs = refs[:slots], refs[slots : 2 * slots]
    held, row_label, row_peak, col_peak, sems = refs[2 * slots :]
    rows = held.shape[1]
    me = my_block()
    copies = [pltpu.make_async_copy(ins[k], held.at[k], sems.at[k]) for k in range(slots)]
    for copy in copies:
        copy.start()
    row_peak[...] = jnp.full(row_peak.shape, EMPTY, jnp.float32)
    col_peak[...] = jnp.full(col_peak.shape, EMPTY, jnp.float32)
    for k in range(slots):
        gid = table_ref[me, k] * rows + lax.broadcasted_iota(jnp.int32, (rows, 128), 0)
        row_label[k] = labels(gid, size_ref, start_ref)
    for copy in copies:
        copy.wait()

    def product(a, b, extra=None):
        sim = lax.dot_general(
            held[a], held[b], (((1,), (1,)), ((), ())), preferred_element_type=jnp.float32
        )
        gid = table_ref[me, b] * rows + lax.broadcasted_iota(jnp.int32, (1, rows), 1)
        lab = labels(gid, size_ref, start_ref)
        mine = jnp.concatenate([row_label[a]] * (rows // 128), axis=1)
        valid = (mine == lab) & (sim > -1.5)
        if extra is not None:
            valid = valid & extra
        sim = jnp.where(valid, sim, jnp.float32(EMPTY))
        best = sim[:, :128]
        for c in range(128, rows, 128):
            best = jnp.maximum(best, sim[:, c : c + 128])
        row_peak[a] = jnp.maximum(row_peak[a], best)
        if extra is None:
            col_peak[b] = jnp.maximum(col_peak[b], jnp.max(sim.reshape(rows // 8, 8, rows), axis=0))

    off = lax.broadcasted_iota(jnp.int32, (rows, rows), 0) != lax.broadcasted_iota(
        jnp.int32, (rows, rows), 1
    )
    product(0, 0, off)

    def body(i, carry):
        product(table_ref[me, slots + 1 + 2 * i], table_ref[me, slots + 2 + 2 * i])
        return carry

    lax.fori_loop(0, table_ref[me, slots], body, 0)
    for k in range(slots):
        across = jnp.max(row_peak[k].T, axis=0, keepdims=True)
        outs[k][...] = jnp.maximum(across, jnp.max(col_peak[k], axis=0, keepdims=True))


def last_kernel(steps, table_ref, live_ref, own_ref, sib_ref, *refs):
    backs, out_ref = refs[:-1], refs[-1]
    me = my_block()
    peak = jnp.maximum(own_ref[...], sib_ref[...])
    for k in range(steps):
        peak = jnp.maximum(peak, jnp.where(table_ref[me, k] == 1, backs[k][...], jnp.float32(EMPTY)))
    out_ref[...] = jnp.where((live_ref[...] == 1) & (peak > -1.5), peak, jnp.float32(0.0))


def per_device(chips, embeddings, cluster_size, cluster_start, live):
    rows, width = embeddings.shape
    steps, table = plan(chips, rows)
    slots = 2 + 2 * len(steps)
    smem = pl.BlockSpec(memory_space=pltpu.SMEM)
    vmem = pl.BlockSpec(memory_space=pltpu.VMEM)
    live = live.reshape(1, rows)
    own = pl.pallas_call(
        norm_kernel,
        out_shape=jax.ShapeDtypeStruct((rows, width), jnp.bfloat16),
        in_specs=[smem, smem, vmem, vmem],
        out_specs=vmem,
        compiler_params=pltpu.CompilerParams(vmem_limit_bytes=32 << 20),
    )(cluster_size, cluster_start, live, embeddings)

    swap = [(d, d ^ 1) for d in range(2 * chips)]
    moves = [[(2 * s + c, 2 * t + c) for s, t in step for c in range(2)] for step in steps]
    sibling = lambda x: lax.ppermute(x, AXES, swap)
    held = [own, sibling(own)]
    for move in moves:
        got = lax.ppermute(own, AXES, move)
        held += [got, sibling(got)]

    peaks = pl.pallas_call(
        functools.partial(pair_kernel, slots),
        out_shape=[jax.ShapeDtypeStruct((1, rows), jnp.float32)] * slots,
        in_specs=[smem] * 3 + [pl.BlockSpec(memory_space=pl.ANY)] * slots,
        out_specs=[vmem] * slots,
        scratch_shapes=[
            pltpu.VMEM((slots, rows, width), jnp.bfloat16),
            pltpu.VMEM((slots, rows, 128), jnp.int32),
            pltpu.VMEM((slots, rows, 128), jnp.float32),
            pltpu.VMEM((slots, 8, rows), jnp.float32),
            pltpu.SemaphoreType.DMA((slots,)),
        ],
        compiler_params=pltpu.CompilerParams(vmem_limit_bytes=48 << 20),
    )(jnp.asarray(table), cluster_size, cluster_start, *held)

    across = sibling(jnp.concatenate(peaks[1::2], axis=0))
    backs = []
    for k, move in enumerate(moves):
        both = jnp.maximum(peaks[2 + 2 * k], across[k + 1 : k + 2])
        backs.append(lax.ppermute(both, AXES, [(t, s) for s, t in move]))
    sent = np.zeros((2 * chips, len(steps)), np.int32)
    for k, move in enumerate(moves):
        for s, _ in move:
            sent[s, k] = 1
    best = pl.pallas_call(
        functools.partial(last_kernel, len(steps)),
        out_shape=jax.ShapeDtypeStruct((1, rows), jnp.float32),
        in_specs=[smem] + [vmem] * (3 + len(steps)),
        out_specs=vmem,
    )(jnp.asarray(sent), live, peaks[0], across[:1], *backs)
    return best.reshape(rows)


def solution(mesh):
    placed = (
        P(("groups", "rows", "cols"), None),
        P("groups"),
        P("groups"),
        P(("groups", "rows", "cols")),
    )
    return jax.shard_map(
        functools.partial(per_device, mesh.shape["rows"]),
        mesh=mesh,
        in_specs=placed,
        out_specs=P(("groups", "rows", "cols")),
        check_vma=False,
    )
```

```python
import functools

import jax
import jax.numpy as jnp
import numpy as np
from jax import lax
from jax.experimental import pallas as pl
from jax.experimental.pallas import tpu as pltpu
from jax.sharding import PartitionSpec as P

AXES = ("rows", "cols")
EMPTY = -2.0
SMEM = pl.BlockSpec(memory_space=pltpu.SMEM)
VMEM = pl.BlockSpec(memory_space=pltpu.VMEM)
ANY = pl.BlockSpec(memory_space=pl.ANY)
HBM = pl.BlockSpec(memory_space=pltpu.HBM)


def layout(chips):
    if chips == 8:
        return 2, [[(0, 2), (1, 0), (2, 3), (3, 1)], [(1, 2), (3, 0)]]
    rounds = [[(c, (c + d) % chips) for c in range(chips)] for d in range(1, (chips + 1) // 2)]
    if chips % 2 == 0:
        rounds.append([(c, c + chips // 2) for c in range(chips // 2)])
    return 1, rounds


def labels(gid, size_ref, start_ref):
    label = jnp.full(gid.shape, -1, jnp.int32)
    for k in range(size_ref.shape[0]):
        first = start_ref[k]
        label = jnp.where((gid >= first) & (gid < first + size_ref[k]), k, label)
    return label


def my_block():
    return lax.axis_index("rows") * lax.axis_size("cols") + lax.axis_index("cols")


def lanes(block, rows):
    return block * rows + lax.broadcasted_iota(jnp.int32, (1, rows), 1)


def norm_kernel(size_hbm, start_hbm, live_hbm, emb_hbm, out_ref, size_ref, start_ref, live_ref, emb_ref, sems):
    pairs = ((emb_hbm, emb_ref), (size_hbm, size_ref), (start_hbm, start_ref), (live_hbm, live_ref))
    copies = [pltpu.make_async_copy(s, d, sems.at[k]) for k, (s, d) in enumerate(pairs)]
    for copy in copies:
        copy.start()
    for copy in copies:
        copy.wait()
    rows, width = emb_ref.shape
    emb = emb_ref[...]
    squares = jnp.sum(emb * emb, axis=1, keepdims=True)
    scale = lax.rsqrt(squares + 1e-06)
    member = labels(lanes(my_block(), rows), size_ref, start_ref) >= 0
    active = jnp.where(member & (live_ref[...] == 1), jnp.float32(1), jnp.float32(0))
    active = jnp.broadcast_to(active, (128, rows)).T[:, :1]
    out_ref[...] = (emb * jnp.where(active > 0, scale, jnp.float32(jnp.nan))).astype(out_ref.dtype)


def products(left, left_label, right, right_label, off=None):
    sim = lax.dot_general(left, right, (((1,), (1,)), ((), ())), preferred_element_type=jnp.float32)
    wide = jnp.concatenate([left_label] * (right_label.shape[1] // 128), axis=1)
    valid = (wide == right_label) & (sim > -1.5)
    if off is not None:
        valid = valid & off
    return jnp.where(valid, sim, jnp.float32(EMPTY))


def fold(sim):
    best = sim[:, :128]
    for c in range(128, sim.shape[1], 128):
        best = jnp.maximum(best, sim[:, c : c + 128])
    return best


def row_labels(block, rows, size_ref, start_ref):
    gid = block * rows + lax.broadcasted_iota(jnp.int32, (rows, 128), 0)
    return labels(gid, size_ref, start_ref)


def column_kernel(n, table_ref, size_ref, start_ref, *refs):
    held, out_ref = refs[:n], refs[n]
    rows = held[0].shape[0]
    me = my_block()
    own = held[0][...]
    mine = row_labels(me, rows, size_ref, start_ref)
    off = lax.broadcasted_iota(jnp.int32, (rows, rows), 0) != lax.broadcasted_iota(
        jnp.int32, (rows, rows), 1
    )
    best = jnp.full((rows, 128), EMPTY, jnp.float32)
    for k in range(n):
        keys = labels(lanes(table_ref[me, k], rows), size_ref, start_ref)
        best = jnp.maximum(best, fold(products(own, mine, held[k][...], keys, off if k == 0 else None)))
    out_ref[...] = jnp.max(best.T, axis=0, keepdims=True)


def visit_kernel(n, slot, first, table_ref, size_ref, start_ref, *refs):
    held, visitor_hbm = refs[:n], refs[n]
    before, refs = refs[n + 1 : 2 * n + 1], refs[2 * n + 1 :]
    if first:
        before = (before[0],)
    outs, back_ref, visitor, sem = refs[:n], refs[n], refs[n + 1], refs[n + 2]
    rows = held[0].shape[0]
    me = my_block()
    copy = pltpu.make_async_copy(visitor_hbm, visitor, sem)
    copy.start()
    theirs = row_labels(table_ref[me, slot], rows, size_ref, start_ref)
    copy.wait()
    best = jnp.full((rows, 128), EMPTY, jnp.float32)
    for k in range(n):
        keys = labels(lanes(table_ref[me, k], rows), size_ref, start_ref)
        sim = products(visitor[...], theirs, held[k][...], keys)
        best = jnp.maximum(best, fold(sim))
        top = jnp.max(sim, axis=0, keepdims=True)
        if k < len(before):
            top = jnp.maximum(top, before[k][...])
        outs[k][...] = top
    back_ref[...] = jnp.max(best.T, axis=0, keepdims=True)


def per_device(chips, embeddings, cluster_size, cluster_start, live):
    rows, width = embeddings.shape
    tall, rounds = layout(chips)
    total = 2 * chips
    devices = 2 * tall
    n = devices
    table = np.full((total, n + len(rounds)), -1, np.int32)
    for d in range(total):
        table[d, :n] = [d ^ k for k in range(n)]
    moves = []
    for r, sends in enumerate(rounds):
        move = [(s * devices + k, t * devices + k) for s, t in sends for k in range(devices)]
        for s, t in move:
            table[t, n + r] = s
        moves.append(move)
    table = jnp.asarray(table)
    params = pltpu.CompilerParams(vmem_limit_bytes=24 << 20)
    small = jax.ShapeDtypeStruct((1, rows), jnp.float32)

    def cost(products, blocks):
        return pl.CostEstimate(
            flops=2 * products * rows * rows * width, bytes_accessed=2 * blocks * rows * width, transcendentals=0
        )

    live = live.reshape(1, rows)
    own = pl.pallas_call(
        norm_kernel,
        out_shape=jax.ShapeDtypeStruct((rows, width), jnp.bfloat16),
        in_specs=[HBM] * 4,
        out_specs=VMEM,
        scratch_shapes=[
            pltpu.SMEM(cluster_size.shape, jnp.int32),
            pltpu.SMEM(cluster_start.shape, jnp.int32),
            pltpu.VMEM((1, rows), jnp.int32),
            pltpu.VMEM((rows, width), jnp.float32),
            pltpu.SemaphoreType.DMA((4,)),
        ],
        compiler_params=pltpu.CompilerParams(vmem_limit_bytes=60 << 20),
    )(cluster_size, cluster_start, live, embeddings)

    def swap(x, k):
        return lax.ppermute(x, AXES, [(d, d ^ k) for d in range(total)])

    visitors = [lax.ppermute(own, AXES, move) for move in moves]
    held = [own, swap(own, 1)]
    if tall == 2:
        across = swap(own, 2)
        across, first = lax.optimization_barrier((across, visitors[0]))
        visitors = [first] + visitors[1:]
        held += [across, swap(across, 1)]

    peaks = [
        pl.pallas_call(
            functools.partial(column_kernel, n),
            out_shape=small,
            in_specs=[SMEM] * 3 + [VMEM] * n,
            out_specs=VMEM,
            compiler_params=params,
            cost_estimate=cost(n, n),
        )(table, cluster_size, cluster_start, *held)
    ]
    backs = []
    for r, (visitor, move) in enumerate(zip(visitors, moves)):
        first = r == 0
        *peaks, back = pl.pallas_call(
            functools.partial(visit_kernel, n, n + r, first),
            out_shape=[small] * (n + 1),
            in_specs=[SMEM] * 3 + [VMEM] * n + [ANY] + [VMEM] * n,
            out_specs=[VMEM] * (n + 1),
            scratch_shapes=[pltpu.VMEM((rows, width), jnp.bfloat16), pltpu.SemaphoreType.DMA],
            compiler_params=params,
            cost_estimate=cost(n, n + 1),
        )(table, cluster_size, cluster_start, *held, visitor, *(peaks * n if first else peaks))
        home = [(t, s) for s, t in move]
        idle = sorted(set(range(total)) - {t for t, _ in home})
        alone = sorted(set(range(total)) - {s for _, s in home})
        backs.append(lax.ppermute(back, AXES, home + list(zip(idle, alone))))

    peak = peaks[0]
    if tall == 2:
        other = swap(jnp.concatenate([peaks[1], peaks[3]], axis=0), 1)
        peak = jnp.maximum(peak, other[:1])
        backs.append(swap(jnp.maximum(peaks[2], other[1:]), 2))
    else:
        backs.append(swap(peaks[1], 1))
    for back in backs:
        peak = jnp.maximum(peak, back)
    return jnp.where((live == 1) & (peak > -1.5), peak, jnp.float32(0.0)).reshape(rows)


def solution(mesh):
    placed = (
        P(("groups", "rows", "cols"), None),
        P("groups"),
        P("groups"),
        P(("groups", "rows", "cols")),
    )
    return jax.shard_map(
        functools.partial(per_device, mesh.shape["rows"]),
        mesh=mesh,
        in_specs=placed,
        out_specs=P(("groups", "rows", "cols")),
        check_vma=False,
    )
```

```python
import functools

import jax
import jax.numpy as jnp
import numpy as np
from jax import lax
from jax.experimental import pallas as pl
from jax.experimental.pallas import tpu as pltpu
from jax.sharding import PartitionSpec as P

AXES = ("rows", "cols")
EMPTY = -2.0
SMEM = pl.BlockSpec(memory_space=pltpu.SMEM)
VMEM = pl.BlockSpec(memory_space=pltpu.VMEM)
ANY = pl.BlockSpec(memory_space=pl.ANY)
HBM = pl.BlockSpec(memory_space=pltpu.HBM)


def layout(chips):
    if chips == 8:
        return 2, [[(0, 2), (1, 0), (2, 3), (3, 1)], [(1, 2), (3, 0)]]
    rounds = [[(c, (c + d) % chips) for c in range(chips)] for d in range(1, (chips + 1) // 2)]
    if chips % 2 == 0:
        rounds.append([(c, c + chips // 2) for c in range(chips // 2)])
    return 1, rounds


def labels(gid, size_ref, start_ref):
    label = jnp.full(gid.shape, -1, jnp.int32)
    for k in range(size_ref.shape[0]):
        first = start_ref[k]
        label = jnp.where((gid >= first) & (gid < first + size_ref[k]), k, label)
    return label


def my_block():
    return lax.axis_index("rows") * lax.axis_size("cols") + lax.axis_index("cols")


def lanes(block, rows):
    return block * rows + lax.broadcasted_iota(jnp.int32, (1, rows), 1)


def norm_kernel(size_hbm, start_hbm, live_hbm, emb_hbm, out_ref, size_ref, start_ref, live_ref, emb_ref, sems):
    pairs = ((emb_hbm, emb_ref), (size_hbm, size_ref), (start_hbm, start_ref), (live_hbm, live_ref))
    copies = [pltpu.make_async_copy(s, d, sems.at[k]) for k, (s, d) in enumerate(pairs)]
    for copy in copies:
        copy.start()
    for copy in copies:
        copy.wait()
    rows, width = emb_ref.shape
    emb = emb_ref[...]
    squares = jnp.sum(emb * emb, axis=1, keepdims=True)
    scale = lax.rsqrt(squares + 1e-06)
    member = labels(lanes(my_block(), rows), size_ref, start_ref) >= 0
    active = jnp.where(member & (live_ref[...] == 1), jnp.float32(1), jnp.float32(0))
    active = jnp.broadcast_to(active, (128, rows)).T[:, :1]
    out_ref[...] = (emb * jnp.where(active > 0, scale, jnp.float32(jnp.nan))).astype(out_ref.dtype)


def products(left, left_label, right, right_label, off=None):
    sim = lax.dot_general(left, right, (((1,), (1,)), ((), ())), preferred_element_type=jnp.float32)
    wide = jnp.concatenate([left_label] * (right_label.shape[1] // 128), axis=1)
    valid = (wide == right_label) & (sim > -1.5)
    if off is not None:
        valid = valid & off
    return jnp.where(valid, sim, jnp.float32(EMPTY))


def fold(sim):
    best = sim[:, :128]
    for c in range(128, sim.shape[1], 128):
        best = jnp.maximum(best, sim[:, c : c + 128])
    return best


def row_labels(block, rows, size_ref, start_ref):
    gid = block * rows + lax.broadcasted_iota(jnp.int32, (rows, 128), 0)
    return labels(gid, size_ref, start_ref)


def blocks_of(refs):
    return [refs[0], refs[1]] + [refs[2].at[lax.axis_index("cols") ^ k] for k in range(2) if len(refs) > 2]


def column_kernel(table_ref, size_ref, start_ref, *refs):
    held, out_ref = blocks_of(refs[:-1]), refs[-1]
    n = len(held)
    rows = held[0].shape[0]
    me = my_block()
    own = held[0][...]
    mine = row_labels(me, rows, size_ref, start_ref)
    off = lax.broadcasted_iota(jnp.int32, (rows, rows), 0) != lax.broadcasted_iota(
        jnp.int32, (rows, rows), 1
    )
    best = jnp.full((rows, 128), EMPTY, jnp.float32)
    for k in range(n):
        keys = labels(lanes(table_ref[me, k], rows), size_ref, start_ref)
        best = jnp.maximum(best, fold(products(own, mine, held[k][...], keys, off if k == 0 else None)))
    out_ref[...] = jnp.max(best.T, axis=0, keepdims=True)


def visit_kernel(n, slot, first, table_ref, size_ref, start_ref, *refs):
    arrays = 2 if n == 2 else 3
    held, visitor_hbm, refs = blocks_of(refs[:arrays]), refs[arrays], refs[arrays + 1 :]
    before, refs = refs[:n], refs[n:]
    if first:
        before = (before[0],)
    outs, back_ref, visitor, sem = refs[:n], refs[n], refs[n + 1], refs[n + 2]
    rows = held[0].shape[0]
    me = my_block()
    copy = pltpu.make_async_copy(visitor_hbm, visitor, sem)
    copy.start()
    theirs = row_labels(table_ref[me, slot], rows, size_ref, start_ref)
    copy.wait()
    best = jnp.full((rows, 128), EMPTY, jnp.float32)
    for k in range(n):
        keys = labels(lanes(table_ref[me, k], rows), size_ref, start_ref)
        sim = products(visitor[...], theirs, held[k][...], keys)
        best = jnp.maximum(best, fold(sim))
        top = jnp.max(sim, axis=0, keepdims=True)
        if k < len(before):
            top = jnp.maximum(top, before[k][...])
        outs[k][...] = top
    back_ref[...] = jnp.max(best.T, axis=0, keepdims=True)


def per_device(chips, embeddings, cluster_size, cluster_start, live):
    rows, width = embeddings.shape
    tall, rounds = layout(chips)
    total = 2 * chips
    devices = 2 * tall
    n = devices
    table = np.full((total, n + len(rounds)), -1, np.int32)
    for d in range(total):
        table[d, :n] = [d ^ k for k in range(n)]
    moves = []
    for r, sends in enumerate(rounds):
        move = [(s * devices + k, t * devices + k) for s, t in sends for k in range(devices)]
        for s, t in move:
            table[t, n + r] = s
        moves.append(move)
    table = jnp.asarray(table)
    params = pltpu.CompilerParams(vmem_limit_bytes=24 << 20)
    small = jax.ShapeDtypeStruct((1, rows), jnp.float32)

    def cost(products, blocks):
        return pl.CostEstimate(
            flops=2 * products * rows * rows * width, bytes_accessed=2 * blocks * rows * width, transcendentals=0
        )

    live = live.reshape(1, rows)
    own = pl.pallas_call(
        norm_kernel,
        out_shape=jax.ShapeDtypeStruct((rows, width), jnp.bfloat16),
        in_specs=[HBM] * 4,
        out_specs=VMEM,
        scratch_shapes=[
            pltpu.SMEM(cluster_size.shape, jnp.int32),
            pltpu.SMEM(cluster_start.shape, jnp.int32),
            pltpu.VMEM((1, rows), jnp.int32),
            pltpu.VMEM((rows, width), jnp.float32),
            pltpu.SemaphoreType.DMA((4,)),
        ],
        compiler_params=pltpu.CompilerParams(vmem_limit_bytes=(63 << 20) + (512 << 10)),
    )(cluster_size, cluster_start, live, embeddings)

    def swap(x, k):
        return lax.ppermute(x, AXES, [(d, d ^ k) for d in range(total)])

    visitors = [lax.ppermute(own, AXES, move) for move in moves]
    held = [own, swap(own, 1)]
    if tall == 2:
        held.append(lax.all_gather(swap(own, 2), "cols"))

    peaks = [
        pl.pallas_call(
            column_kernel,
            out_shape=small,
            in_specs=[SMEM] * 3 + [VMEM] * len(held),
            out_specs=VMEM,
            compiler_params=params,
            cost_estimate=cost(n, n),
        )(table, cluster_size, cluster_start, *held)
    ]
    backs = []
    for r, (visitor, move) in enumerate(zip(visitors, moves)):
        first = r == 0
        *peaks, back = pl.pallas_call(
            functools.partial(visit_kernel, n, n + r, first),
            out_shape=[small] * (n + 1),
            in_specs=[SMEM] * 3 + [VMEM] * len(held) + [ANY] + [VMEM] * n,
            out_specs=[VMEM] * (n + 1),
            scratch_shapes=[pltpu.VMEM((rows, width), jnp.bfloat16), pltpu.SemaphoreType.DMA],
            compiler_params=params,
            cost_estimate=cost(n, n + 1),
        )(table, cluster_size, cluster_start, *held, visitor, *(peaks * n if first else peaks))
        home = [(t, s) for s, t in move]
        idle = sorted(set(range(total)) - {t for t, _ in home})
        alone = sorted(set(range(total)) - {s for _, s in home})
        backs.append(lax.ppermute(back, AXES, home + list(zip(idle, alone))))

    peak = peaks[0]
    if tall == 2:
        other = swap(jnp.concatenate([peaks[1], peaks[3]], axis=0), 1)
        peak = jnp.maximum(peak, other[:1])
        backs.append(swap(jnp.maximum(peaks[2], other[1:]), 2))
    else:
        backs.append(swap(peaks[1], 1))
    for back in backs:
        peak = jnp.maximum(peak, back)
    return jnp.where((live == 1) & (peak > -1.5), peak, jnp.float32(0.0)).reshape(rows)


def solution(mesh):
    placed = (
        P(("groups", "rows", "cols"), None),
        P("groups"),
        P("groups"),
        P(("groups", "rows", "cols")),
    )
    return jax.shard_map(
        functools.partial(per_device, mesh.shape["rows"]),
        mesh=mesh,
        in_specs=placed,
        out_specs=P(("groups", "rows", "cols")),
        check_vma=False,
    )
```

```python
import functools

import jax
import jax.numpy as jnp
import numpy as np
from jax import lax
from jax.experimental import pallas as pl
from jax.experimental.pallas import tpu as pltpu
from jax.sharding import PartitionSpec as P

AXES = ("rows", "cols")
EMPTY = -2.0
SMEM = pl.BlockSpec(memory_space=pltpu.SMEM)
VMEM = pl.BlockSpec(memory_space=pltpu.VMEM)
HBM = pl.BlockSpec(memory_space=pltpu.HBM)


def layout(chips):
    if chips == 8:
        return 2, [[(0, 2), (1, 0), (2, 3), (3, 1)], [(1, 2), (3, 0)]]
    rounds = [[(c, (c + d) % chips) for c in range(chips)] for d in range(1, (chips + 1) // 2)]
    if chips % 2 == 0:
        rounds.append([(c, c + chips // 2) for c in range(chips // 2)])
    return 1, rounds


def labels(gid, size_ref, start_ref):
    label = jnp.full(gid.shape, -1, jnp.int32)
    for k in range(size_ref.shape[0]):
        first = start_ref[k]
        label = jnp.where((gid >= first) & (gid < first + size_ref[k]), k, label)
    return label


def my_block():
    return lax.axis_index("rows") * lax.axis_size("cols") + lax.axis_index("cols")


def lanes(block, rows):
    return block * rows + lax.broadcasted_iota(jnp.int32, (1, rows), 1)


def norm_kernel(size_hbm, start_hbm, live_hbm, emb_hbm, out_ref, size_ref, start_ref, live_ref, emb_ref, sems):
    pairs = ((emb_hbm, emb_ref), (size_hbm, size_ref), (start_hbm, start_ref), (live_hbm, live_ref))
    copies = [pltpu.make_async_copy(s, d, sems.at[k]) for k, (s, d) in enumerate(pairs)]
    for copy in copies:
        copy.start()
    for copy in copies:
        copy.wait()
    rows, width = emb_ref.shape
    emb = emb_ref[...]
    squares = jnp.sum(emb * emb, axis=1, keepdims=True)
    scale = lax.rsqrt(squares + 1e-06)
    member = labels(lanes(my_block(), rows), size_ref, start_ref) >= 0
    active = jnp.where(member & (live_ref[...] == 1), jnp.float32(1), jnp.float32(0))
    active = jnp.broadcast_to(active, (128, rows)).T[:, :1]
    out_ref[...] = (emb * jnp.where(active > 0, scale, jnp.float32(jnp.nan))).astype(out_ref.dtype)


def products(left, left_label, right, right_label, off=None):
    sim = lax.dot_general(left, right, (((1,), (1,)), ((), ())), preferred_element_type=jnp.float32)
    wide = jnp.concatenate([left_label] * (right_label.shape[1] // 128), axis=1)
    valid = (wide == right_label) & (sim > -1.5)
    if off is not None:
        valid = valid & off
    return jnp.where(valid, sim, jnp.float32(EMPTY))


def fold(sim):
    best = sim[:, :128]
    for c in range(128, sim.shape[1], 128):
        best = jnp.maximum(best, sim[:, c : c + 128])
    return best


def row_labels(block, rows, size_ref, start_ref):
    gid = block * rows + lax.broadcasted_iota(jnp.int32, (rows, 128), 0)
    return labels(gid, size_ref, start_ref)


def blocks_of(refs):
    blocks = []
    for ref in refs:
        if len(ref.shape) == 2:
            blocks.append(ref)
        else:
            blocks += [ref.at[lax.axis_index("cols") ^ k] for k in range(2)]
    return blocks


def column_kernel(table_ref, size_ref, start_ref, before_ref, *refs):
    held, out_ref = blocks_of(refs[:-1]), refs[-1]
    n = len(held)
    rows = held[0].shape[0]
    me = my_block()
    own = held[0][...]
    mine = row_labels(me, rows, size_ref, start_ref)
    off = lax.broadcasted_iota(jnp.int32, (rows, rows), 0) != lax.broadcasted_iota(
        jnp.int32, (rows, rows), 1
    )
    best = jnp.full((rows, 128), EMPTY, jnp.float32)
    for k in range(n):
        keys = labels(lanes(table_ref[me, k], rows), size_ref, start_ref)
        best = jnp.maximum(best, fold(products(own, mine, held[k][...], keys, off if k == 0 else None)))
    out_ref[...] = jnp.maximum(before_ref[...], jnp.max(best.T, axis=0, keepdims=True))


def visit_kernel(ids, slot, blocks, befores, table_ref, size_ref, start_ref, visitor, *refs):
    n = len(ids)
    held, refs = blocks_of(refs[:blocks]), refs[blocks:]
    before, (*outs, back_ref) = refs[:befores], refs[befores:]
    rows = visitor.shape[0]
    me = my_block()
    theirs = row_labels(table_ref[me, slot], rows, size_ref, start_ref)
    best = jnp.full((rows, 128), EMPTY, jnp.float32)
    for k in range(n):
        keys = labels(lanes(table_ref[me, ids[k]], rows), size_ref, start_ref)
        sim = products(visitor[...], theirs, held[k][...], keys)
        best = jnp.maximum(best, fold(sim))
        top = jnp.max(sim, axis=0, keepdims=True)
        outs[k][...] = jnp.maximum(top, before[k][...]) if befores else top
    back_ref[...] = jnp.max(best.T, axis=0, keepdims=True)


def per_device(chips, embeddings, cluster_size, cluster_start, live):
    rows, width = embeddings.shape
    tall, rounds = layout(chips)
    total = 2 * chips
    devices = 2 * tall
    n = devices
    table = np.full((total, n + len(rounds)), -1, np.int32)
    for d in range(total):
        table[d, :n] = [d ^ k for k in range(n)]
    moves = []
    for r, sends in enumerate(rounds):
        move = [(s * devices + k, t * devices + k) for s, t in sends for k in range(devices)]
        for s, t in move:
            table[t, n + r] = s
        moves.append(move)
    table = jnp.asarray(table)
    params = pltpu.CompilerParams(vmem_limit_bytes=24 << 20)
    small = jax.ShapeDtypeStruct((1, rows), jnp.float32)

    def cost(products, blocks):
        return pl.CostEstimate(
            flops=2 * products * rows * rows * width, bytes_accessed=2 * blocks * rows * width, transcendentals=0
        )

    live = live.reshape(1, rows)
    own = pl.pallas_call(
        norm_kernel,
        out_shape=jax.ShapeDtypeStruct((rows, width), jnp.bfloat16),
        in_specs=[HBM] * 4,
        out_specs=VMEM,
        scratch_shapes=[
            pltpu.SMEM(cluster_size.shape, jnp.int32),
            pltpu.SMEM(cluster_start.shape, jnp.int32),
            pltpu.VMEM((1, rows), jnp.int32),
            pltpu.VMEM((rows, width), jnp.float32),
            pltpu.SemaphoreType.DMA((4,)),
        ],
        compiler_params=pltpu.CompilerParams(vmem_limit_bytes=(63 << 20) + (512 << 10)),
    )(cluster_size, cluster_start, live, embeddings)

    def swap(x, k):
        return lax.ppermute(x, AXES, [(d, d ^ k) for d in range(total)])

    visitors = [lax.ppermute(own, AXES, move) for move in moves]
    def visit(r, ids, held, before):
        *peaks, back = pl.pallas_call(
            functools.partial(visit_kernel, ids, n + r, len(held), len(before)),
            out_shape=[small] * (len(ids) + 1),
            in_specs=[SMEM] * 3 + [VMEM] * (1 + len(held) + len(before)),
            out_specs=[VMEM] * (len(ids) + 1),
            compiler_params=params,
            cost_estimate=cost(len(ids), len(ids) + 1),
        )(table, cluster_size, cluster_start, visitors[r], *held, *before)
        return peaks, back

    held = [own, swap(own, 1)]
    peaks, back = visit(0, (0, 1), held, [])
    if tall == 2:
        across, *peaks = lax.optimization_barrier((swap(own, 2), *peaks))
        held.append(lax.all_gather(across, "cols"))
        more, rest = visit(0, (2, 3), held[2:], [])
        peaks, back = peaks + more, jnp.maximum(back, rest)

    peaks[0] = pl.pallas_call(
        column_kernel,
        out_shape=small,
        in_specs=[SMEM] * 3 + [VMEM] * (1 + len(held)),
        out_specs=VMEM,
        compiler_params=params,
        cost_estimate=cost(n, n),
    )(table, cluster_size, cluster_start, peaks[0], *held)
    backs = []
    for r, move in enumerate(moves):
        if r:
            peaks, back = visit(r, tuple(range(n)), held, peaks)
        home = [(t, s) for s, t in move]
        idle = sorted(set(range(total)) - {t for t, _ in home})
        alone = sorted(set(range(total)) - {s for _, s in home})
        backs.append(lax.ppermute(back, AXES, home + list(zip(idle, alone))))

    peak = peaks[0]
    if tall == 2:
        other = swap(jnp.concatenate([peaks[1], peaks[3]], axis=0), 1)
        peak = jnp.maximum(peak, other[:1])
        backs.append(swap(jnp.maximum(peaks[2], other[1:]), 2))
    else:
        backs.append(swap(peaks[1], 1))
    for back in backs:
        peak = jnp.maximum(peak, back)
    return jnp.where(peak > -1.5, peak, jnp.float32(0.0)).reshape(rows)


def solution(mesh):
    placed = (
        P(("groups", "rows", "cols"), None),
        P("groups"),
        P("groups"),
        P(("groups", "rows", "cols")),
    )
    return jax.shard_map(
        functools.partial(per_device, mesh.shape["rows"]),
        mesh=mesh,
        in_specs=placed,
        out_specs=P(("groups", "rows", "cols")),
        check_vma=False,
    )
```

```python
import functools

import jax
import jax.numpy as jnp
import numpy as np
from jax import lax
from jax.experimental import pallas as pl
from jax.experimental.pallas import tpu as pltpu
from jax.sharding import PartitionSpec as P

AXES = ("rows", "cols")
EMPTY = -2.0
SMEM = pl.BlockSpec(memory_space=pltpu.SMEM)
VMEM = pl.BlockSpec(memory_space=pltpu.VMEM)
HBM = pl.BlockSpec(memory_space=pltpu.HBM)


def layout(chips):
    if chips == 8:
        return 2, [[(0, 2), (1, 0), (2, 3), (3, 1)], [(1, 2), (3, 0)]]
    rounds = [[(c, (c + d) % chips) for c in range(chips)] for d in range(1, (chips + 1) // 2)]
    if chips % 2 == 0:
        rounds.append([(c, c + chips // 2) for c in range(chips // 2)])
    return 1, rounds


def labels(gid, size_ref, start_ref):
    label = jnp.full(gid.shape, -1, jnp.int32)
    for k in range(size_ref.shape[0]):
        first = start_ref[k]
        label = jnp.where((gid >= first) & (gid < first + size_ref[k]), k, label)
    return label


def my_block():
    return lax.axis_index("rows") * lax.axis_size("cols") + lax.axis_index("cols")


def lanes(block, rows):
    return block * rows + lax.broadcasted_iota(jnp.int32, (1, rows), 1)


def norm_kernel(size_hbm, start_hbm, live_hbm, emb_hbm, out_ref, size_ref, start_ref, live_ref, emb_ref, sems):
    pairs = ((emb_hbm, emb_ref), (size_hbm, size_ref), (start_hbm, start_ref), (live_hbm, live_ref))
    copies = [pltpu.make_async_copy(s, d, sems.at[k]) for k, (s, d) in enumerate(pairs)]
    for copy in copies:
        copy.start()
    for copy in copies:
        copy.wait()
    rows, width = emb_ref.shape
    emb = emb_ref[...]
    squares = jnp.sum(emb * emb, axis=1, keepdims=True)
    scale = lax.rsqrt(squares + 1e-06)
    member = labels(lanes(my_block(), rows), size_ref, start_ref) >= 0
    active = jnp.where(member & (live_ref[...] == 1), jnp.float32(1), jnp.float32(0))
    active = jnp.broadcast_to(active, (128, rows)).T[:, :1]
    out_ref[...] = (emb * jnp.where(active > 0, scale, jnp.float32(jnp.nan))).astype(out_ref.dtype)


def products(left, left_label, right, right_label, off=None):
    sim = lax.dot_general(left, right, (((1,), (1,)), ((), ())), preferred_element_type=jnp.float32)
    wide = jnp.concatenate([left_label] * (right_label.shape[1] // 128), axis=1)
    valid = (wide == right_label) & (sim > -1.5)
    if off is not None:
        valid = valid & off
    return jnp.where(valid, sim, jnp.float32(EMPTY))


def fold(sim):
    best = sim[:, :128]
    for c in range(128, sim.shape[1], 128):
        best = jnp.maximum(best, sim[:, c : c + 128])
    return best


def row_labels(block, rows, size_ref, start_ref):
    gid = block * rows + lax.broadcasted_iota(jnp.int32, (rows, 128), 0)
    return labels(gid, size_ref, start_ref)


def blocks_of(refs):
    return [ref.at[lax.axis_index("cols") ^ k] for ref in refs for k in range(2)]


def meet_kernel(ids, lefts, blocks, tops_before, rows_before, table_ref, size_ref, start_ref, *refs):
    left_refs, refs = refs[: len(lefts)], refs[len(lefts) :]
    left_refs = [blocks_of([ref])[0] if len(ref.shape) == 3 else ref for ref in left_refs]
    held, refs = blocks_of(refs[:blocks]), refs[blocks:]
    befores, outs = refs[: tops_before + rows_before], refs[tops_before + rows_before :]
    rows = left_refs[0].shape[0]
    me = my_block()
    keys = [labels(lanes(table_ref[me, k], rows), size_ref, start_ref) for k in ids]
    tops = len(ids) if lefts[0] else 0
    for n, (slot, left) in enumerate(zip(lefts, left_refs)):
        mine = row_labels(table_ref[me, slot], rows, size_ref, start_ref)
        best = jnp.full((rows, 128), EMPTY, jnp.float32)
        for k, (block, key) in enumerate(zip(held, keys)):
            off = None
            if slot == ids[k]:
                off = lax.broadcasted_iota(jnp.int32, (rows, rows), 0) != lax.broadcasted_iota(
                    jnp.int32, (rows, rows), 1
                )
            sim = products(left[...], mine, block[...], key, off)
            best = jnp.maximum(best, fold(sim))
            if n == 0 and tops:
                top = jnp.max(sim, axis=0, keepdims=True)
                outs[k][...] = jnp.maximum(top, befores[k][...]) if k < tops_before else top
        best = jnp.max(best.T, axis=0, keepdims=True)
        if rows_before:
            best = jnp.maximum(best, befores[tops_before + n][...])
        outs[tops + n][...] = best


def per_device(chips, embeddings, cluster_size, cluster_start, live):
    rows, width = embeddings.shape
    tall, rounds = layout(chips)
    total = 2 * chips
    devices = 2 * tall
    n = devices
    table = np.full((total, n + len(rounds)), -1, np.int32)
    for d in range(total):
        table[d, :n] = [d ^ k for k in range(n)]
    moves = []
    for r, sends in enumerate(rounds):
        move = [(s * devices + k, t * devices + k) for s, t in sends for k in range(devices)]
        for s, t in move:
            table[t, n + r] = s
        moves.append(move)
    table = jnp.asarray(table)
    params = pltpu.CompilerParams(vmem_limit_bytes=24 << 20)
    small = jax.ShapeDtypeStruct((1, rows), jnp.float32)

    def cost(products, blocks):
        return pl.CostEstimate(
            flops=2 * products * rows * rows * width, bytes_accessed=2 * blocks * rows * width, transcendentals=0
        )

    live = live.reshape(1, rows)
    own = pl.pallas_call(
        norm_kernel,
        out_shape=jax.ShapeDtypeStruct((rows, width), jnp.bfloat16),
        in_specs=[HBM] * 4,
        out_specs=VMEM,
        scratch_shapes=[
            pltpu.SMEM(cluster_size.shape, jnp.int32),
            pltpu.SMEM(cluster_start.shape, jnp.int32),
            pltpu.VMEM((1, rows), jnp.int32),
            pltpu.VMEM((rows, width), jnp.float32),
            pltpu.SemaphoreType.DMA((4,)),
        ],
        compiler_params=pltpu.CompilerParams(vmem_limit_bytes=(63 << 20) + (512 << 10)),
    )(cluster_size, cluster_start, live, embeddings)

    def swap(x, k):
        return lax.ppermute(x, AXES, [(d, d ^ k) for d in range(total)])

    visitors = [lax.ppermute(own, AXES, move) for move in moves]
    def meet(ids, lefts, held, tops=(), rows_=()):
        slots, blocks = zip(*lefts)
        args = [*blocks, *held, *tops, *rows_]
        outs = (len(ids) if slots[0] else 0) + len(lefts)
        got = pl.pallas_call(
            functools.partial(meet_kernel, ids, slots, len(held), len(tops), len(rows_)),
            out_shape=[small] * outs,
            in_specs=[SMEM] * 3 + [VMEM] * len(args),
            out_specs=[VMEM] * outs,
            compiler_params=params,
            cost_estimate=cost(len(ids) * len(lefts), len(ids) + len(lefts)),
        )(table, cluster_size, cluster_start, *args)
        return got[: outs - len(lefts)], got[outs - len(lefts) :]

    held = [lax.all_gather(own, "cols")]
    _, mine = meet((0, 1), [(0, held[0])], held)
    peaks, (back,) = meet((0, 1), [(n, visitors[0])], held, mine)
    if tall == 2:
        across, *peaks = lax.optimization_barrier((swap(own, 2), *peaks))
        held.append(lax.all_gather(across, "cols"))
        more, (back, mine) = meet((2, 3), [(n, visitors[0]), (0, held[0])], held[1:], (), (back, peaks[0]))
        peaks = [mine, *peaks[1:], *more]

    backs = []
    for r, move in enumerate(moves):
        if r:
            peaks, (back,) = meet(tuple(range(n)), [(n + r, visitors[r])], held, peaks)
        home = [(t, s) for s, t in move]
        idle = sorted(set(range(total)) - {t for t, _ in home})
        alone = sorted(set(range(total)) - {s for _, s in home})
        back = lax.ppermute(back, AXES, home + list(zip(idle, alone)))
        if False:
            back, peaks = lax.optimization_barrier((back, peaks))
        backs.append(back)

    peak = peaks[0]
    if tall == 2:
        other = swap(jnp.concatenate([peaks[1], peaks[3]], axis=0), 1)
        peak = jnp.maximum(peak, other[:1])
        backs.append(swap(jnp.maximum(peaks[2], other[1:]), 2))
    else:
        backs.append(swap(peaks[1], 1))
    for back in backs:
        peak = jnp.maximum(peak, back)
    return jnp.where(peak > -1.5, peak, jnp.float32(0.0)).reshape(rows)


def solution(mesh):
    placed = (
        P(("groups", "rows", "cols"), None),
        P("groups"),
        P("groups"),
        P(("groups", "rows", "cols")),
    )
    return jax.shard_map(
        functools.partial(per_device, mesh.shape["rows"]),
        mesh=mesh,
        in_specs=placed,
        out_specs=P(("groups", "rows", "cols")),
        check_vma=False,
    )
```

```python
import functools

import jax
import jax.numpy as jnp
import numpy as np
from jax import lax
from jax.experimental import pallas as pl
from jax.experimental.pallas import tpu as pltpu
from jax.sharding import PartitionSpec as P

AXES = ("rows", "cols")
EMPTY = -2.0
SMEM = pl.BlockSpec(memory_space=pltpu.SMEM)
VMEM = pl.BlockSpec(memory_space=pltpu.VMEM)
HBM = pl.BlockSpec(memory_space=pltpu.HBM)


def layout(chips):
    if chips == 8:
        return 2, [[(0, 2), (1, 0), (2, 3), (3, 1)], [(1, 2), (3, 0)]]
    rounds = [[(c, (c + d) % chips) for c in range(chips)] for d in range(1, (chips + 1) // 2)]
    if chips % 2 == 0:
        rounds.append([(c, c + chips // 2) for c in range(chips // 2)])
    return 1, rounds


def labels(gid, size_ref, start_ref):
    label = jnp.full(gid.shape, -1, jnp.int32)
    for k in range(size_ref.shape[0]):
        first = start_ref[k]
        label = jnp.where((gid >= first) & (gid < first + size_ref[k]), k, label)
    return label


def my_block():
    return lax.axis_index("rows") * lax.axis_size("cols") + lax.axis_index("cols")


def lanes(block, rows):
    return block * rows + lax.broadcasted_iota(jnp.int32, (1, rows), 1)


def norm_kernel(size_hbm, start_hbm, live_hbm, emb_hbm, out_ref, size_ref, start_ref, live_ref, emb_ref, sems):
    pairs = ((emb_hbm, emb_ref), (size_hbm, size_ref), (start_hbm, start_ref), (live_hbm, live_ref))
    copies = [pltpu.make_async_copy(s, d, sems.at[k]) for k, (s, d) in enumerate(pairs)]
    for copy in copies:
        copy.start()
    for copy in copies:
        copy.wait()
    rows, width = emb_ref.shape
    emb = emb_ref[...]
    squares = jnp.sum(emb * emb, axis=1, keepdims=True)
    scale = lax.rsqrt(squares + 1e-06)
    member = labels(lanes(my_block(), rows), size_ref, start_ref) >= 0
    active = jnp.where(member & (live_ref[...] == 1), jnp.float32(1), jnp.float32(0))
    active = jnp.broadcast_to(active, (128, rows)).T[:, :1]
    out_ref[...] = (emb * jnp.where(active > 0, scale, jnp.float32(jnp.nan))).astype(out_ref.dtype)


def products(left, left_label, right, right_label, off=None):
    sim = lax.dot_general(left, right, (((1,), (1,)), ((), ())), preferred_element_type=jnp.float32)
    wide = jnp.concatenate([left_label] * (right_label.shape[1] // 128), axis=1)
    valid = (wide == right_label) & (sim > -1.5)
    if off is not None:
        valid = valid & off
    return jnp.where(valid, sim, jnp.float32(EMPTY))


def fold(sim):
    best = sim[:, :128]
    for c in range(128, sim.shape[1], 128):
        best = jnp.maximum(best, sim[:, c : c + 128])
    return best


def row_labels(block, rows, size_ref, start_ref):
    gid = block * rows + lax.broadcasted_iota(jnp.int32, (rows, 128), 0)
    return labels(gid, size_ref, start_ref)


def blocks_of(refs):
    return [ref.at[lax.axis_index("cols") ^ k] for ref in refs for k in range(2)]


def meet_kernel(ids, lefts, blocks, tops_before, rows_before, table_ref, size_ref, start_ref, *refs):
    left_refs, refs = refs[: len(lefts)], refs[len(lefts) :]
    left_refs = [blocks_of([ref])[0] if len(ref.shape) == 3 else ref for ref in left_refs]
    held, refs = blocks_of(refs[:blocks]), refs[blocks:]
    befores, outs = refs[: tops_before + rows_before], refs[tops_before + rows_before :]
    rows = left_refs[0].shape[0]
    me = my_block()
    keys = [labels(lanes(table_ref[me, k], rows), size_ref, start_ref) for k in ids]
    tops = len(ids) if lefts[0] else 0
    for n, (slot, left) in enumerate(zip(lefts, left_refs)):
        mine = row_labels(table_ref[me, slot], rows, size_ref, start_ref)
        best = jnp.full((rows, 128), EMPTY, jnp.float32)
        for k, (block, key) in enumerate(zip(held, keys)):
            off = None
            if slot == ids[k]:
                off = lax.broadcasted_iota(jnp.int32, (rows, rows), 0) != lax.broadcasted_iota(
                    jnp.int32, (rows, rows), 1
                )
            sim = products(left[...], mine, block[...], key, off)
            best = jnp.maximum(best, fold(sim))
            if n == 0 and tops:
                top = jnp.max(sim, axis=0, keepdims=True)
                outs[k][...] = jnp.maximum(top, befores[k][...]) if k < tops_before else top
        best = jnp.max(best.T, axis=0, keepdims=True)
        if rows_before:
            best = jnp.maximum(best, befores[tops_before + n][...])
        outs[tops + n][...] = best


def per_device(chips, embeddings, cluster_size, cluster_start, live):
    rows, width = embeddings.shape
    tall, rounds = layout(chips)
    total = 2 * chips
    devices = 2 * tall
    n = devices
    table = np.full((total, n + len(rounds)), -1, np.int32)
    for d in range(total):
        table[d, :n] = [d ^ k for k in range(n)]
    moves = []
    for r, sends in enumerate(rounds):
        move = [(s * devices + k, t * devices + k) for s, t in sends for k in range(devices)]
        for s, t in move:
            table[t, n + r] = s
        moves.append(move)
    table = jnp.asarray(table)
    params = pltpu.CompilerParams(vmem_limit_bytes=24 << 20)
    small = jax.ShapeDtypeStruct((1, rows), jnp.float32)

    def cost(products, blocks):
        return pl.CostEstimate(
            flops=2 * products * rows * rows * width, bytes_accessed=2 * blocks * rows * width, transcendentals=0
        )

    live = live.reshape(1, rows)
    own = pl.pallas_call(
        norm_kernel,
        out_shape=jax.ShapeDtypeStruct((rows, width), jnp.bfloat16),
        in_specs=[HBM] * 4,
        out_specs=VMEM,
        scratch_shapes=[
            pltpu.SMEM(cluster_size.shape, jnp.int32),
            pltpu.SMEM(cluster_start.shape, jnp.int32),
            pltpu.VMEM((1, rows), jnp.int32),
            pltpu.VMEM((rows, width), jnp.float32),
            pltpu.SemaphoreType.DMA((4,)),
        ],
        compiler_params=pltpu.CompilerParams(vmem_limit_bytes=(63 << 20) + (512 << 10)),
    )(cluster_size, cluster_start, live, embeddings)

    def swap(x, k):
        return lax.ppermute(x, AXES, [(d, d ^ k) for d in range(total)])

    visitors = [lax.ppermute(own, AXES, move) for move in moves]
    def meet(ids, lefts, held, tops=(), rows_=()):
        slots, blocks = zip(*lefts)
        args = [*blocks, *held, *tops, *rows_]
        outs = (len(ids) if slots[0] else 0) + len(lefts)
        got = pl.pallas_call(
            functools.partial(meet_kernel, ids, slots, len(held), len(tops), len(rows_)),
            out_shape=[small] * outs,
            in_specs=[SMEM] * 3 + [VMEM] * len(args),
            out_specs=[VMEM] * outs,
            compiler_params=params,
            cost_estimate=cost(len(ids) * len(lefts), len(ids) + len(lefts)),
        )(table, cluster_size, cluster_start, *args)
        return got[: outs - len(lefts)], got[outs - len(lefts) :]

    held = [lax.all_gather(own, "cols")]
    _, mine = meet((0, 1), [(0, held[0])], held)
    peaks, (back,) = meet((0, 1), [(n, visitors[0])], held, mine)
    if tall == 2:
        across, *peaks = lax.optimization_barrier((swap(own, 2), *peaks))
        held.append(lax.all_gather(across, "cols"))
        more, (back, mine) = meet((2, 3), [(n, visitors[0]), (0, held[0])], held[1:], (), (back, peaks[0]))
        peaks = [mine, *peaks[1:], *more]

    backs = []
    for r, move in enumerate(moves):
        if r:
            peaks, (back,) = meet(tuple(range(n)), [(n + r, visitors[r])], held, peaks)
        home = [(t, s) for s, t in move]
        idle = sorted(set(range(total)) - {t for t, _ in home})
        alone = sorted(set(range(total)) - {s for _, s in home})
        backs.append(lax.ppermute(back, AXES, home + list(zip(idle, alone))))
    backs[0], peaks = lax.optimization_barrier((backs[0], peaks))

    peak = peaks[0]
    if tall == 2:
        other = swap(jnp.concatenate([peaks[1], peaks[3]], axis=0), 1)
        peak = jnp.maximum(peak, other[:1])
        backs.append(swap(jnp.maximum(peaks[2], other[1:]), 2))
    else:
        backs.append(swap(peaks[1], 1))
    for back in backs:
        peak = jnp.maximum(peak, back)
    return jnp.where(peak > -1.5, peak, jnp.float32(0.0)).reshape(rows)


def solution(mesh):
    placed = (
        P(("groups", "rows", "cols"), None),
        P("groups"),
        P("groups"),
        P(("groups", "rows", "cols")),
    )
    return jax.shard_map(
        functools.partial(per_device, mesh.shape["rows"]),
        mesh=mesh,
        in_specs=placed,
        out_specs=P(("groups", "rows", "cols")),
        check_vma=False,
    )
```

```python
import functools

import jax
import jax.numpy as jnp
import numpy as np
from jax import lax
from jax.experimental import pallas as pl
from jax.experimental.pallas import tpu as pltpu
from jax.sharding import PartitionSpec as P

AXES = ("rows", "cols")
EMPTY = -2.0
SMEM = pl.BlockSpec(memory_space=pltpu.SMEM)
VMEM = pl.BlockSpec(memory_space=pltpu.VMEM)
HBM = pl.BlockSpec(memory_space=pltpu.HBM)


def layout(chips):
    if chips == 8:
        return 2, [[(0, 2), (1, 0), (2, 3), (3, 1)], [(2, 1), (0, 3)]]
    rounds = [[(c, (c + d) % chips) for c in range(chips)] for d in range(1, (chips + 1) // 2)]
    if chips % 2 == 0:
        rounds.append([(c, c + chips // 2) for c in range(chips // 2)])
    return 1, rounds


def labels(gid, size_ref, start_ref):
    label = jnp.full(gid.shape, -1, jnp.int32)
    for k in range(size_ref.shape[0]):
        first = start_ref[k]
        label = jnp.where((gid >= first) & (gid < first + size_ref[k]), k, label)
    return label


def my_block():
    return lax.axis_index("rows") * lax.axis_size("cols") + lax.axis_index("cols")


def lanes(block, rows):
    return block * rows + lax.broadcasted_iota(jnp.int32, (1, rows), 1)


def norm_kernel(size_hbm, start_hbm, live_hbm, emb_hbm, out_ref, size_ref, start_ref, live_ref, emb_ref, sems):
    pairs = ((emb_hbm, emb_ref), (size_hbm, size_ref), (start_hbm, start_ref), (live_hbm, live_ref))
    copies = [pltpu.make_async_copy(s, d, sems.at[k]) for k, (s, d) in enumerate(pairs)]
    for copy in copies:
        copy.start()
    for copy in copies:
        copy.wait()
    rows, width = emb_ref.shape
    emb = emb_ref[...]
    squares = jnp.sum(emb * emb, axis=1, keepdims=True)
    scale = lax.rsqrt(squares + 1e-06)
    member = labels(lanes(my_block(), rows), size_ref, start_ref) >= 0
    active = jnp.where(member & (live_ref[...] == 1), jnp.float32(1), jnp.float32(0))
    active = jnp.broadcast_to(active, (128, rows)).T[:, :1]
    out_ref[...] = (emb * jnp.where(active > 0, scale, jnp.float32(jnp.nan))).astype(out_ref.dtype)


def products(left, left_label, right, right_label, off=None):
    sim = lax.dot_general(left, right, (((1,), (1,)), ((), ())), preferred_element_type=jnp.float32)
    wide = jnp.concatenate([left_label] * (right_label.shape[1] // 128), axis=1)
    valid = (wide == right_label) & (sim > -1.5)
    if off is not None:
        valid = valid & off
    return jnp.where(valid, sim, jnp.float32(EMPTY))


def fold(sim):
    best = sim[:, :128]
    for c in range(128, sim.shape[1], 128):
        best = jnp.maximum(best, sim[:, c : c + 128])
    return best


def row_labels(block, rows, size_ref, start_ref):
    gid = block * rows + lax.broadcasted_iota(jnp.int32, (rows, 128), 0)
    return labels(gid, size_ref, start_ref)


def blocks_of(refs):
    return [ref.at[lax.axis_index("cols") ^ k] for ref in refs for k in range(2)]


def meet_kernel(ids, lefts, blocks, tops_before, rows_before, table_ref, size_ref, start_ref, *refs):
    left_refs, refs = refs[: len(lefts)], refs[len(lefts) :]
    left_refs = [blocks_of([ref])[0] if len(ref.shape) == 3 else ref for ref in left_refs]
    held, refs = blocks_of(refs[:blocks]), refs[blocks:]
    befores, outs = refs[: tops_before + rows_before], refs[tops_before + rows_before :]
    rows = left_refs[0].shape[0]
    me = my_block()
    keys = [labels(lanes(table_ref[me, k], rows), size_ref, start_ref) for k in ids]
    tops = len(ids) if lefts[0] else 0
    for n, (slot, left) in enumerate(zip(lefts, left_refs)):
        mine = row_labels(table_ref[me, slot], rows, size_ref, start_ref)
        best = jnp.full((rows, 128), EMPTY, jnp.float32)
        for k, (block, key) in enumerate(zip(held, keys)):
            off = None
            if slot == ids[k]:
                off = lax.broadcasted_iota(jnp.int32, (rows, rows), 0) != lax.broadcasted_iota(
                    jnp.int32, (rows, rows), 1
                )
            sim = products(left[...], mine, block[...], key, off)
            best = jnp.maximum(best, fold(sim))
            if n == 0 and tops:
                top = jnp.max(sim, axis=0, keepdims=True)
                outs[k][...] = jnp.maximum(top, befores[k][...]) if k < tops_before else top
        best = jnp.max(best.T, axis=0, keepdims=True)
        if rows_before:
            best = jnp.maximum(best, befores[tops_before + n][...])
        outs[tops + n][...] = best


def per_device(chips, embeddings, cluster_size, cluster_start, live):
    rows, width = embeddings.shape
    tall, rounds = layout(chips)
    total = 2 * chips
    devices = 2 * tall
    n = devices
    table = np.full((total, n + len(rounds)), -1, np.int32)
    for d in range(total):
        table[d, :n] = [d ^ k for k in range(n)]
    moves = []
    for r, sends in enumerate(rounds):
        move = [(s * devices + k, t * devices + k) for s, t in sends for k in range(devices)]
        for s, t in move:
            table[t, n + r] = s
        moves.append(move)
    table = jnp.asarray(table)
    params = pltpu.CompilerParams(vmem_limit_bytes=24 << 20)
    small = jax.ShapeDtypeStruct((1, rows), jnp.float32)

    def cost(products, blocks):
        return pl.CostEstimate(
            flops=2 * products * rows * rows * width, bytes_accessed=2 * blocks * rows * width, transcendentals=0
        )

    live = live.reshape(1, rows)
    own = pl.pallas_call(
        norm_kernel,
        out_shape=jax.ShapeDtypeStruct((rows, width), jnp.bfloat16),
        in_specs=[HBM] * 4,
        out_specs=VMEM,
        scratch_shapes=[
            pltpu.SMEM(cluster_size.shape, jnp.int32),
            pltpu.SMEM(cluster_start.shape, jnp.int32),
            pltpu.VMEM((1, rows), jnp.int32),
            pltpu.VMEM((rows, width), jnp.float32),
            pltpu.SemaphoreType.DMA((4,)),
        ],
        compiler_params=pltpu.CompilerParams(vmem_limit_bytes=(63 << 20) + (512 << 10)),
    )(cluster_size, cluster_start, live, embeddings)

    def swap(x, k):
        return lax.ppermute(x, AXES, [(d, d ^ k) for d in range(total)])

    visitors = [lax.ppermute(own, AXES, move) for move in moves]
    def meet(ids, lefts, held, tops=(), rows_=()):
        slots, blocks = zip(*lefts)
        args = [*blocks, *held, *tops, *rows_]
        outs = (len(ids) if slots[0] else 0) + len(lefts)
        got = pl.pallas_call(
            functools.partial(meet_kernel, ids, slots, len(held), len(tops), len(rows_)),
            out_shape=[small] * outs,
            in_specs=[SMEM] * 3 + [VMEM] * len(args),
            out_specs=[VMEM] * outs,
            compiler_params=params,
            cost_estimate=cost(len(ids) * len(lefts), len(ids) + len(lefts)),
        )(table, cluster_size, cluster_start, *args)
        return got[: outs - len(lefts)], got[outs - len(lefts) :]

    held = [lax.all_gather(own, "cols")]
    _, mine = meet((0, 1), [(0, held[0])], held)
    peaks, (back,) = meet((0, 1), [(n, visitors[0])], held, mine)
    if tall == 2:
        across, *peaks = lax.optimization_barrier((swap(own, 2), *peaks))
        held.append(lax.all_gather(across, "cols"))
        more, (back,) = meet((2, 3), [(n, visitors[0])], held[1:], (), (back,))
        peaks += more

    backs = []
    for r, move in enumerate(moves):
        if r:
            peaks, (back,) = meet(tuple(range(n)), [(n + r, visitors[r])], held, peaks)
        home = [(t, s) for s, t in move]
        idle = sorted(set(range(total)) - {t for t, _ in home})
        alone = sorted(set(range(total)) - {s for _, s in home})
        backs.append(lax.ppermute(back, AXES, home + list(zip(idle, alone))))
    backs[0], peaks = lax.optimization_barrier((backs[0], peaks))

    peak = peaks[0]
    if tall == 2:
        _, mine = meet((2, 3), [(0, held[0])], held[1:])
        peak = jnp.maximum(peak, mine[0])
        other = swap(jnp.concatenate([peaks[1], peaks[3]], axis=0), 1)
        peak = jnp.maximum(peak, other[:1])
        backs.append(swap(jnp.maximum(peaks[2], other[1:]), 2))
    else:
        backs.append(swap(peaks[1], 1))
    for back in backs:
        peak = jnp.maximum(peak, back)
    return jnp.where(peak > -1.5, peak, jnp.float32(0.0)).reshape(rows)


def solution(mesh):
    placed = (
        P(("groups", "rows", "cols"), None),
        P("groups"),
        P("groups"),
        P(("groups", "rows", "cols")),
    )
    return jax.shard_map(
        functools.partial(per_device, mesh.shape["rows"]),
        mesh=mesh,
        in_specs=placed,
        out_specs=P(("groups", "rows", "cols")),
        check_vma=False,
    )
```
